512 devices in a mesh: island: 8 (over y, x_hi), fsdp: 64 (over z, x_lo, core).
Axes of the slice: x: 4 (x_hi: 2, x_lo: 2; x = x_hi * 2 + x_lo), y: 4, z: 16, core: 2. Of those that a mesh axis runs over, the one named last changes fastest.
Arguments:
- activations: bfloat16 [8, 2, 16384, 4096], P('island', None, 'fsdp'), may hold values from -500 to 500, as said below
- cotangent: bfloat16 [8, 2, 16384, 128], P('island', None, 'fsdp'), may hold values from -6 to 6
- island_params: float32 [8, 4096, 256], P('island', 'fsdp'), may hold values from -6 to 6
- first_moment: float32 [8, 4096, 256], P('island', 'fsdp'), may hold values from -4 to 4
- second_moment: float32 [8, 4096, 256], P('island', 'fsdp'), may hold values from 0.01 to 1
- anchor: float32 [4096, 256], P('fsdp'), may hold values from -6 to 6
- momentum: float32 [4096, 256], P('fsdp'), may hold values from -4 to 4
Outputs:
- new_anchor: float32 [4096, 256], P('fsdp')
- new_momentum: float32 [4096, 256], P('fsdp')
- new_first: float32 [8, 4096, 256], P('island', 'fsdp')
- new_second: float32 [8, 4096, 256], P('island', 'fsdp')
The draws below stay inside these ranges and needn't reach their ends.
Inputs may be any that keep to these rules, and one draw needn't show every extreme that they name: `activations`: finite layer inputs.
All inputs are finite; a program needn't handle non-finite values.
Results may differ from the reference program's by a relative error of at most 0.0003.
Values sent between devices are 32-bit elements; how exact they have to be, the bound alone decides.
A program may use at most 64 MiB of HBM per device.

```python
import math
import jax
import jax.numpy as jnp
from jax import lax

D = 4096
HD = 128
LAYERS = 2
ISLANDS = 8
TOK_ISLAND = 16384


def draw_activations(key, part):
    key = jax.random.fold_in(key, 11)
    key_cols, key_rows, key_base = jax.random.split(key, 3)
    column_scale = 10.0 ** (jnp.arange(D, dtype=jnp.float32) / D) * jax.random.uniform(key_cols, (D,), jnp.float32, 0.8, 1.25)
    row_scale = 10.0 ** jax.random.uniform(key_rows, (ISLANDS, LAYERS, TOK_ISLAND, 1), jnp.float32, 0.0, 1.0)
    base = jax.random.normal(key_base, (ISLANDS, LAYERS, TOK_ISLAND, D), jnp.float32)
    base = jnp.clip(base, -4.0, 4.0)
    return (base * row_scale * column_scale).astype(jnp.bfloat16)


def level_of(own_key, extent, shards, least, largest):
    gain = 1.0
    for position, shards_of in shards:
        steps = jax.random.uniform(jax.random.fold_in(jax.random.fold_in(own_key, 6), position), (shards_of,), jnp.float32, least / len(shards), largest / len(shards))
        gain = gain * jnp.repeat(jnp.exp(steps), extent[position] // shards_of).reshape((-1,) + (1,) * (len(extent) - 1 - position))
    return gain


def noise(rng, extent, deviation, most, cuts=(), kind=jnp.bfloat16):
    result = jax.random.normal(rng, extent, jnp.float32) * deviation
    if len(cuts) > 0:
        result = level_of(rng, extent, cuts, -0.22, 0.18) * result
    return jnp.clip(result, min=-most, max=most).astype(kind)


def setup_inputs(seed: int = 0) -> dict:
    key_of = jax.random.split(jax.random.key(seed), 8)
    return {
        "activations": draw_activations(jax.random.fold_in(key_of[7], 71), 0),
        "cotangent": noise(key_of[1], (ISLANDS, LAYERS, TOK_ISLAND, HD), 1.0, 6.0, ((0, 8), (2, 64))),
        "island_params": noise(key_of[2], (ISLANDS, D, LAYERS * HD), 1.0, 6.0, ((0, 8), (1, 64)), jnp.float32),
        "first_moment": noise(key_of[3], (ISLANDS, D, LAYERS * HD), 0.3, 4.0, ((0, 8), (1, 64)), jnp.float32),
        "second_moment": jnp.clip(jnp.exp(math.log(1.0) - 4.6051702 * jax.random.uniform(key_of[4], (ISLANDS, D, LAYERS * HD), jnp.float32) ** level_of(key_of[4], (ISLANDS, D, LAYERS * HD), ((0, 8), (1, 64)), -0.2, 0.2)), 0.01, 1.0),
        "anchor": noise(key_of[5], (D, LAYERS * HD), 1.0, 6.0, ((0, 64),), jnp.float32),
        "momentum": noise(key_of[6], (D, LAYERS * HD), 0.3, 4.0, ((0, 64),), jnp.float32),
    }


def island_gradient(island_pair):
    island_inputs, island_outputs = island_pair
    blocks = []
    for layer_index in range(LAYERS):
        blocks.append(lax.dot_general(island_inputs[layer_index], island_outputs[layer_index], (((0,), (0,)), ((), ())), preferred_element_type=jnp.float32))
    return jnp.concatenate(blocks, axis=1)

def reference(activations, cotangent, island_params, first_moment, second_moment, anchor, momentum):
    gradient = lax.map(island_gradient, (activations, cotangent))
    squares = lax.optimization_barrier(jnp.sum(gradient * gradient, axis=(1, 2), keepdims=True))
    clip_limit = 0.5 * jnp.sqrt(jnp.float32(D * LAYERS * HD))
    factor = jnp.minimum(1.0, clip_limit / (jnp.sqrt(squares) + 1e-06))
    clipped = factor * gradient
    new_first = 0.9 * first_moment + 0.1 * clipped
    new_second = 0.95 * second_moment + 0.05 * clipped * clipped
    stepped = island_params - 0.05 * (new_first / (jnp.sqrt(new_second) + 1e-08) + 0.1 * island_params)
    drift = anchor[None] - stepped
    mean_drift = lax.optimization_barrier(jnp.sum(drift, axis=0)) / ISLANDS
    new_momentum = 0.9 * momentum + mean_drift
    new_anchor = anchor - 0.7 * (mean_drift + 0.9 * new_momentum)
    return (new_anchor, new_momentum, new_first, new_second)
```

```python
import functools

import jax
import jax.numpy as jnp
from jax import lax
from jax.experimental import pallas as pl
from jax.experimental.pallas import tpu as pltpu
from jax.sharding import PartitionSpec as P

MESH = pl.DeviceIdType.MESH
F32 = jnp.float32
RX = 104
RC = 128 - RX


def kernel(nz, ni, clip_limit, act, cot, par, fm, sm, anc, o_cl, o_md,
           a_v, c_v, ct, pp, h, pr, xv, ar, al, cr, cl, xz, gt, gs, gb, ssl, dr, drr, md, st, res,
           ld_sem, cs, cr_sem, xs, xr, rs, rr, ms, mr, ss_s, ss_r, is_s, is_r, os):
    half = nz // 2
    i, f = lax.axis_index("island"), lax.axis_index("fsdp")
    z, x, c = f // 4, (f // 2) % 2, f % 2
    ox, oc = 1 - x, 1 - c
    rows = 64 // ni

    def dev(dz=0, xx=None, cc=None):
        zz = lax.rem(z + dz + nz, nz)
        return (i, zz * 4 + (x if xx is None else xx) * 2 + (c if cc is None else cc))

    def copy(src, dst, s, r, to):
        return pltpu.make_async_remote_copy(src_ref=src, dst_ref=dst, send_sem=s, recv_sem=r, device_id=to, device_id_type=MESH)

    barrier = pltpu.get_barrier_semaphore()

    def offset(k):
        return (2 * (k % 2) - 1) * (half - (k + 1) // 2)

    def load(k):
        zk = lax.rem(z + offset(k) + nz, nz)
        return pltpu.make_async_copy(act.at[0, :, :, pl.ds(pl.multiple_of(zk * 256, 256), 256)], a_v.at[k], ld_sem.at[k])

    def at_k(o):
        return 0 if abs(o) == half else 2 * (half - abs(o)) - (1 if o > 0 else 0)

    load_c = pltpu.make_async_copy(cot.at[0], c_v, ld_sem.at[nz])
    load_c.start()
    lax.fori_loop(0, nz, lambda k, _: (load(k).start(), 0)[1], 0)
    state = [pltpu.make_async_copy(src, st.at[n], ld_sem.at[nz + 1 + n])
             for n, src in enumerate((par.at[0], fm.at[0], sm.at[0], anc))]
    for s in state:
        s.start()

    near = [dev(cc=oc), dev(xx=ox), dev(1), dev(-1), dev(2), dev(-2)]
    for to in near:
        pl.semaphore_signal(barrier, inc=1, device_id=to, device_id_type=MESH)

    def greet_islands(n, _):
        pl.semaphore_signal(barrier, inc=1, device_id=(lax.rem(i + n, ni), f), device_id_type=MESH)
        return 0

    lax.fori_loop(1, ni, greet_islands, 0)

    load_c.wait()
    for l in range(2):
        ct[l] = c_v[l].T

    def core_copy(k):
        return copy(pp.at[k], pr.at[k], cs.at[k], cr_sem.at[k], dev(cc=oc))

    def x_copy(k):
        return copy(h.at[k, ox, 0:RX], xv.at[k], xs.at[k], xr.at[k], dev(xx=ox))

    def product(k):
        load(k).wait()
        for l, out in ((oc, pp), (c, h)):
            p = jnp.dot(ct[l], a_v[k, l], preferred_element_type=F32)
            out[k, 0] = p[:, :128]
            out[k, 1] = p[:, 128:]

    def core_sum(k):
        core_copy(k).wait_recv()
        h[k] += pr[k]
        x_copy(k).start()

    product(0)
    pl.semaphore_wait(barrier, len(near) + ni - 1)
    core_copy(0).start()

    streams = {"ar": (0, 1, ar), "al": (1, -1, al), "cr": (2, 1, cr), "cl": (3, -1, cl)}

    def ring(name, o):
        n, sign, buf = streams[name]
        k = at_k(sign * o)
        src = h.at[k, x, 0:RX] if name[0] == "a" else h.at[k, :, RX:128]
        return copy(src, buf.at[o], rs.at[n, o], rr.at[n, o], dev(dz=sign * (2 - o % 2)))

    def a_add(k, name, o):
        longest = half if name in ("ar", "cl") else half - 1
        buf = streams[name][2]
        total = None
        for d in (o + 2, o + 1):
            if d <= longest and (d % 2 or d == o + 2):
                ring(name, d).wait_recv()
                total = buf[d] if total is None else total + buf[d]
        return total

    def chain_a(name, o):
        k = at_k(streams[name][1] * o)
        x_copy(k).wait_recv()
        t = h[k, x, 0:RX] + xv[k]
        if o % 2 == 0 and o < half:
            t = t + a_add(k, name, o)
        h[k, x, 0:RX] = t
        ring(name, o).start()

    def chain_c(name, o):
        if o % 2 == 0 and o < half:
            k = at_k(streams[name][1] * o)
            h[k, :, RX:128] += a_add(k, name, o)
        ring(name, o).start()

    def group(g):
        return [0] if g == 0 else ([nz - 1] if g == half else [2 * g - 1, 2 * g])

    def produce(g):
        for k in group(g):
            product(k)
            core_copy(k).start()

    def collect(g):
        for k in group(g):
            core_sum(k)
        if g == 0:
            chain_c("cl", half)
        elif (half - g) % 2:
            chain_c("cr", half - g)
            chain_c("cl", half - g)

    produce(1)
    collect(0)
    for g in range(2, half + 1):
        produce(g)
        collect(g - 1)
    collect(half)

    chain_a("ar", half)
    for o in range(half - 1, 0, -1):
        if o % 2:
            chain_a("ar", o)
            chain_a("al", o)
        else:
            chain_c("cr", o)
            chain_c("cl", o)
            chain_a("ar", o)
            chain_a("al", o)
        if o == 2:
            last = nz - 1
            h[last, :, RX:128] += a_add(last, "cr", 0) + a_add(last, "cl", 0)
            zx = copy(h.at[last, ox, RX:128], xz, ms.at[0], mr.at[0], dev(xx=ox))
            zx.start()
    x_copy(last).wait_recv()
    gt[0:RX] = h[last, x, 0:RX] + xv[last] + a_add(last, "ar", 0) + a_add(last, "al", 0)
    zx.wait_recv()
    gt[RX:128] = h[last, x, RX:128] + xz[...]

    g = gt[...]
    ssl[0] = jnp.sum(g * g, axis=0, keepdims=True)

    def ss_copy(n):
        return copy(ssl.at[0], ssl.at[n], ss_s.at[n], ss_r.at[n], (i, lax.rem(f + n, 4 * nz)))

    def ss_start(n, _):
        ss_copy(2 * nz + n).start()
        ss_copy(2 * nz - n).start()
        return 0

    ss_copy(2 * nz).start()
    lax.fori_loop(1, 2 * nz, ss_start, 0)

    gt[...] = g.T
    gs[...] = gt[pl.ds(pl.multiple_of(oc * 64, 64), 64)]
    gx = copy(gs, gb.at[c], ms.at[1], mr.at[1], dev(cc=oc))
    gx.start()
    gb[c] = gt[pl.ds(pl.multiple_of(c * 64, 64), 64)]
    for s in state:
        s.wait()
    gx.wait_recv()

    def ss_wait(n, _):
        ss_copy(n).wait_recv()
        return 0

    lax.fori_loop(1, 4 * nz, ss_wait, 0)
    squares = jnp.sum(jnp.sum(ssl[...], axis=0), axis=-1, keepdims=True)
    factor = jnp.minimum(1.0, clip_limit / (jnp.sqrt(squares) + 1e-06))

    for l in range(2):
        col = slice(l * 128, (l + 1) * 128)
        clipped = factor * gb[l]
        nf = 0.9 * st[1, :, col] + 0.1 * clipped
        ns = 0.95 * st[2, :, col] + 0.05 * clipped * clipped
        p = st[0, :, col]
        stepped = p - 0.05 * (nf / (jnp.sqrt(ns) + 1e-08) + 0.1 * p)
        dr[:, col] = st[3, :, col] - stepped
        res[:, col] = clipped

    outs = [pltpu.make_async_copy(src, dst, os.at[n]) for n, (src, dst) in enumerate(((res, o_cl), (md, o_md)))]

    mine = pl.ds(pl.multiple_of(i * rows, rows), rows)

    def to_island(n):
        return (lax.rem(i + n, ni), f)

    def dr_copy(n):
        j = lax.rem(i + n, ni)
        return copy(dr.at[pl.ds(pl.multiple_of(j * rows, rows), rows)], drr.at[n], is_s.at[0, n], is_r.at[0, n], to_island(n))

    def md_copy(n):
        return copy(md.at[mine], md.at[mine], is_s.at[1, n], is_r.at[1, n], to_island(n))

    for n in range(1, ni):
        dr_copy(n).start()
    outs[0].start()
    total = dr[mine]
    for n in range(1, ni):
        dr_copy(n).wait_recv()
        total = total + drr[n]
    md[mine] = total / ni
    for n in range(1, ni):
        md_copy(n).start()
    for n in range(1, ni):
        md_copy(n).wait_recv()
    outs[1].start()

    def sent_k(k, _):
        core_copy(k).wait_send()
        x_copy(k).wait_send()
        return 0

    lax.fori_loop(0, nz, sent_k, 0)
    for name, longest in (("ar", half), ("al", half - 1), ("cr", half - 1), ("cl", half)):
        for o in range(1, longest + 1):
            ring(name, o).wait_send()
    zx.wait_send()
    gx.wait_send()

    def sent_ss(n, _):
        ss_copy(n).wait_send()
        return 0

    lax.fori_loop(1, 4 * nz, sent_ss, 0)
    for n in range(1, ni):
        dr_copy(n).wait_send()
        md_copy(n).wait_send()
    for o in outs:
        o.wait()


def shards(act, cot, par, fm, sm, anc, mom):
    nf, ni = lax.axis_size("fsdp"), lax.axis_size("island")
    nz = nf // 4
    half = nz // 2
    tok = act.shape[2]
    limit = 0.5 * float(act.shape[3] * 256) ** 0.5
    hbm = pl.BlockSpec(memory_space=pl.ANY)
    vm, dma = pltpu.VMEM, pltpu.SemaphoreType.DMA
    clipped, mean_drift = pl.pallas_call(
        functools.partial(kernel, nz, ni, limit),
        out_shape=[jax.ShapeDtypeStruct(anc.shape, F32)] * 2,
        in_specs=[hbm] * 6,
        out_specs=[hbm] * 2,
        scratch_shapes=[
            vm((nz, 2, tok, 256), jnp.bfloat16), vm((2, tok, 128), jnp.bfloat16), vm((2, 128, tok), jnp.bfloat16),
            vm((nz, 2, 128, 128), F32), vm((nz, 2, 128, 128), F32), vm((nz, 2, 128, 128), F32),
            vm((nz, RX, 128), F32),
            vm((half + 1, RX, 128), F32), vm((half + 1, RX, 128), F32),
            vm((half + 1, 2, RC, 128), F32), vm((half + 1, 2, RC, 128), F32),
            vm((RC, 128), F32), vm((128, 128), F32), vm((64, 128), F32), vm((2, 64, 128), F32),
            vm((nf, 1, 128), F32),
            vm((64, 256), F32), vm((ni, 64 // ni, 256), F32), vm((64, 256), F32),
            vm((4, 64, 256), F32), vm((64, 256), F32),
            dma((nz + 5,)), dma((nz,)), dma((nz,)), dma((nz,)), dma((nz,)),
            dma((4, half + 1)), dma((4, half + 1)), dma((2,)), dma((2,)),
            dma((nf,)), dma((nf,)), dma((2, ni)), dma((2, ni)), dma((2,)),
        ],
        compiler_params=pltpu.CompilerParams(collective_id=0, has_side_effects=True, vmem_limit_bytes=62 << 20),
    )(act, cot, par, fm, sm, anc)
    new_first = 0.9 * fm[0] + 0.1 * clipped
    new_second = 0.95 * sm[0] + 0.05 * clipped * clipped
    new_mom = 0.9 * mom + mean_drift
    new_anc = anc - 0.7 * (mean_drift + 0.9 * new_mom)
    return new_anc, new_mom, new_first[None], new_second[None]


def solution(mesh):
    return jax.shard_map(
        shards,
        mesh=mesh,
        in_specs=(
            P("island", None, "fsdp", None),
            P("island", None, "fsdp", None),
            P("island", "fsdp", None),
            P("island", "fsdp", None),
            P("island", "fsdp", None),
            P("fsdp", None),
            P("fsdp", None),
        ),
        out_specs=(
            P("fsdp", None),
            P("fsdp", None),
            P("island", "fsdp", None),
            P("island", "fsdp", None),
        ),
        check_vma=False,
    )
```

```python
import functools

import jax
import jax.numpy as jnp
from jax import lax
from jax.experimental import pallas as pl
from jax.experimental.pallas import tpu as pltpu
from jax.sharding import PartitionSpec as P

MESH = pl.DeviceIdType.MESH
F32 = jnp.float32
STREAMS = ((0, 56, True, 1), (56, 112, True, -1), (112, 128, False, -1))
PRE, LAG, PA, PB, PC = 2, 3, 4, 6, 7
RX = 112
RC = 128 - RX


def kernel(nz, ni, clip_limit, act, cot, par, fm, sm, anc, o_cl, o_md,
           a_v, c_v, ct, pp, h, pr, xv, ring_a, ring_c, xz, gt, gs, gb, ssl, dr, drr, md, st, res,
           word, ld_sem, cs, cr_sem, xs, xr, rs, rr, ms, mr, ss_s, ss_r, is_s, is_r, os):
    half = nz // 2
    i, f = lax.axis_index("island"), lax.axis_index("fsdp")
    z, x, c = f // 4, (f // 2) % 2, f % 2
    ox, oc = 1 - x, 1 - c
    rows = 64 // ni

    def dev(dz=0, xx=None, cc=None):
        zz = lax.rem(z + dz + nz, nz)
        return (i, zz * 4 + (x if xx is None else xx) * 2 + (c if cc is None else cc))

    def copy(src, dst, s, r, to):
        return pltpu.make_async_remote_copy(src_ref=src, dst_ref=dst, send_sem=s, recv_sem=r, device_id=to, device_id_type=MESH)

    barrier = pltpu.get_barrier_semaphore()

    def offset(k):
        return (2 * (k % 2) - 1) * (half - (k + 1) // 2)

    def load(k):
        zk = lax.rem(z + offset(k) + nz, nz)
        return pltpu.make_async_copy(act.at[0, :, :, pl.ds(pl.multiple_of(zk * 256, 256), 256)], a_v.at[k], ld_sem.at[k])

    def at_k(o):
        return 0 if abs(o) == half else 2 * (half - abs(o)) - (1 if o > 0 else 0)

    load_c = pltpu.make_async_copy(cot.at[0], c_v, ld_sem.at[nz])
    load_c.start()
    lax.fori_loop(0, nz, lambda k, _: (load(k).start(), 0)[1], 0)
    state = [pltpu.make_async_copy(src, st.at[n], ld_sem.at[nz + 1 + n])
             for n, src in enumerate((par.at[0], fm.at[0], sm.at[0], anc))]
    for s in state:
        s.start()

    yy, xp = i // 2, 2 * lax.rem(i, 2) + x

    def beside(dy, dx, dz):
        xq = lax.rem(xp + dx + 4, 4)
        return (lax.rem(yy + dy + ni // 2, ni // 2) * 2 + xq // 2, lax.rem(z + dz + nz, nz) * 4 + lax.rem(xq, 2) * 2 + c)

    sides = [beside(1, 0, 0), beside(-1, 0, 0), beside(0, 1, 0), beside(0, -1, 0), beside(0, 0, 1), beside(0, 0, -1)]
    for to in sides + [dev(cc=oc)]:
        pl.semaphore_signal(barrier, inc=1, device_id=to, device_id_type=MESH)

    def tell(r, which):
        for d in which:
            pl.semaphore_signal(word.at[r, d], inc=1, device_id=sides[d], device_id_type=MESH)

    def hear(r, which):
        for d in which:
            pl.semaphore_wait(word.at[r, d], 1)

    load_c.wait()
    for l in range(2):
        ct[l] = c_v[l].T

    first_x = [n for n, t in enumerate(STREAMS) if t[2]]
    last_x = [n for n, t in enumerate(STREAMS) if not t[2]]

    def core_copy(k):
        return copy(pp.at[k], pr.at[k], cs.at[k], cr_sem.at[k], dev(cc=oc))

    def x_copy(k, n):
        lo, hi = STREAMS[n][:2]
        return copy(h.at[k, ox, lo:hi], xv.at[k, lo:hi], xs.at[n, k], xr.at[n, k], dev(xx=ox))

    def product(k):
        load(k).wait()
        for l, out in ((oc, pp), (c, h)):
            p = jnp.dot(ct[l], a_v[k, l], preferred_element_type=F32)
            out[k, 0] = p[:, :128]
            out[k, 1] = p[:, 128:]

    def core_sum(k):
        core_copy(k).wait_recv()
        h[k] += pr[k]
        for n in first_x:
            x_copy(k, n).start()

    early = 2 * PRE + 1
    for k in range(early):
        product(k)
    pl.semaphore_wait(barrier, len(sides) + 1)
    tell(0, range(6))
    for k in range(early):
        core_copy(k).start()

    def longest(n, sign):
        return half if sign == STREAMS[n][3] else half - 1

    def landed(n, sign, o):
        lo, hi, first, _ = STREAMS[n]
        d = (sign + 1) // 2
        return ring_a.at[d, o, lo:hi] if first else ring_c.at[d, o, :, lo - RX:hi - RX]

    def ring(n, sign, o):
        lo, hi, first, _ = STREAMS[n]
        k = at_k(sign * o)
        d = (sign + 1) // 2
        src = h.at[k, x, lo:hi] if first else h.at[k, :, lo:hi]
        return copy(src, landed(n, sign, o), rs.at[n, d, o], rr.at[n, d, o], dev(dz=sign * (2 - o % 2)))

    def come(n, sign, o):
        total = None
        for d in (o + 2, o + 1):
            if d <= longest(n, sign):
                ring(n, sign, d).wait_recv()
                part = landed(n, sign, d)[...]
                total = part if total is None else total + part
        return total

    def pass_on(n, sign, o):
        lo, hi, first, _ = STREAMS[n]
        if o > longest(n, sign):
            return
        k = at_k(sign * o)
        t = come(n, sign, o) if o % 2 == 0 else None
        if first:
            x_copy(k, n).wait_recv()
            own = h[k, x, lo:hi] + xv[k, lo:hi]
            h[k, x, lo:hi] = own if t is None else own + t
        elif t is not None:
            h[k, :, lo:hi] += t
        ring(n, sign, o).start()

    def pass_all(which, o):
        for n in which:
            for sign in (1, -1):
                pass_on(n, sign, o)

    def group(g):
        return [0] if g == 0 else ([nz - 1] if g == half else [2 * g - 1, 2 * g])

    def produce(g):
        for k in group(g):
            if k >= early:
                product(k)
                core_copy(k).start()

    def collect(g):
        for k in group(g):
            core_sum(k)
        if g == 0:
            hear(0, (4, 5))
        if g == 0 or (half - g) % 2:
            pass_all(last_x, half - g)

    for g in range(1, LAG + 1):
        produce(g)
    for g in range(half + 1):
        collect(g)
        if g + LAG < half:
            produce(g + LAG + 1)
        if g == PA:
            pass_all(first_x, half)
        if g == PC:
            pass_all(last_x, half - 2)
        if g == PB:
            pass_all(first_x, half - 1)

    hear(0, range(4))
    tell(1, range(4))
    last = nz - 1
    zx = [copy(h.at[last, ox, STREAMS[n][0]:STREAMS[n][1]], xz.at[STREAMS[n][0] - RX:STREAMS[n][1] - RX],
               ms.at[2 + n], mr.at[2 + n], dev(xx=ox)) for n in last_x]
    for o in range(half - 2, 0, -1):
        if o == half // 2:
            hear(1, range(4))
            tell(2, range(4))
        if o % 2 == 0 and o < half - 2:
            pass_all(last_x, o)
        pass_all(first_x, o)
        if o == 2:
            for j, n in enumerate(last_x):
                lo, hi = STREAMS[n][:2]
                h[last, :, lo:hi] += come(n, 1, 0) + come(n, -1, 0)
                zx[j].start()
    for n in first_x:
        lo, hi = STREAMS[n][:2]
        x_copy(last, n).wait_recv()
        gt[lo:hi] = h[last, x, lo:hi] + xv[last, lo:hi] + come(n, 1, 0) + come(n, -1, 0)
    for c_x in zx:
        c_x.wait_recv()
    gt[RX:128] = h[last, x, RX:128] + xz[...]

    g = gt[...]
    ssl[0] = jnp.sum(g * g, axis=0, keepdims=True)

    def ss_copy(n):
        return copy(ssl.at[0], ssl.at[n], ss_s.at[n], ss_r.at[n], (i, lax.rem(f + n, 4 * nz)))

    def ss_start(n, _):
        ss_copy(2 * nz + n).start()
        ss_copy(2 * nz - n).start()
        return 0

    ss_copy(2 * nz).start()
    lax.fori_loop(1, 2 * nz, ss_start, 0)

    hear(2, range(4))
    gt[...] = g.T
    gs[...] = gt[pl.ds(pl.multiple_of(oc * 64, 64), 64)]
    gx = copy(gs, gb.at[c], ms.at[1], mr.at[1], dev(cc=oc))
    gx.start()
    gb[c] = gt[pl.ds(pl.multiple_of(c * 64, 64), 64)]
    for s in state:
        s.wait()
    gx.wait_recv()

    def ss_wait(n, _):
        ss_copy(n).wait_recv()
        return 0

    lax.fori_loop(1, 4 * nz, ss_wait, 0)
    squares = jnp.sum(jnp.sum(ssl[...], axis=0), axis=-1, keepdims=True)
    factor = jnp.minimum(1.0, clip_limit / (jnp.sqrt(squares) + 1e-06))

    for l in range(2):
        col = slice(l * 128, (l + 1) * 128)
        clipped = factor * gb[l]
        nf = 0.9 * st[1, :, col] + 0.1 * clipped
        ns = 0.95 * st[2, :, col] + 0.05 * clipped * clipped
        p = st[0, :, col]
        stepped = p - 0.05 * (nf / (jnp.sqrt(ns) + 1e-08) + 0.1 * p)
        dr[:, col] = st[3, :, col] - stepped
        res[:, col] = clipped

    outs = [pltpu.make_async_copy(src, dst, os.at[n]) for n, (src, dst) in enumerate(((res, o_cl), (md, o_md)))]

    mine = pl.ds(pl.multiple_of(i * rows, rows), rows)

    def to_island(n):
        return (lax.rem(i + n, ni), f)

    def dr_copy(n):
        j = lax.rem(i + n, ni)
        return copy(dr.at[pl.ds(pl.multiple_of(j * rows, rows), rows)], drr.at[n], is_s.at[0, n], is_r.at[0, n], to_island(n))

    def md_copy(n):
        return copy(md.at[mine], md.at[mine], is_s.at[1, n], is_r.at[1, n], to_island(n))

    for n in range(1, ni):
        dr_copy(n).start()
    outs[0].start()
    total = dr[mine]
    for n in range(1, ni):
        dr_copy(n).wait_recv()
        total = total + drr[n]
    md[mine] = total / ni
    for n in range(1, ni):
        md_copy(n).start()
    for n in range(1, ni):
        md_copy(n).wait_recv()
    outs[1].start()

    def sent_k(k, _):
        core_copy(k).wait_send()
        for n in first_x:
            x_copy(k, n).wait_send()
        return 0

    lax.fori_loop(0, nz, sent_k, 0)
    for n in range(len(STREAMS)):
        for sign in (1, -1):
            for o in range(1, longest(n, sign) + 1):
                ring(n, sign, o).wait_send()
    for c_x in zx:
        c_x.wait_send()
    gx.wait_send()

    def sent_ss(n, _):
        ss_copy(n).wait_send()
        return 0

    lax.fori_loop(1, 4 * nz, sent_ss, 0)
    for n in range(1, ni):
        dr_copy(n).wait_send()
        md_copy(n).wait_send()
    for o in outs:
        o.wait()


def shards(act, cot, par, fm, sm, anc, mom):
    nf, ni = lax.axis_size("fsdp"), lax.axis_size("island")
    nz = nf // 4
    half = nz // 2
    tok = act.shape[2]
    limit = 0.5 * float(act.shape[3] * 256) ** 0.5
    hbm = pl.BlockSpec(memory_space=pl.ANY)
    ns = len(STREAMS)
    vm, dma = pltpu.VMEM, pltpu.SemaphoreType.DMA
    clipped, mean_drift = pl.pallas_call(
        functools.partial(kernel, nz, ni, limit),
        out_shape=[jax.ShapeDtypeStruct(anc.shape, F32)] * 2,
        in_specs=[hbm] * 6,
        out_specs=[hbm] * 2,
        scratch_shapes=[
            vm((nz, 2, tok, 256), jnp.bfloat16), vm((2, tok, 128), jnp.bfloat16), vm((2, 128, tok), jnp.bfloat16),
            vm((nz, 2, 128, 128), F32), vm((nz, 2, 128, 128), F32), vm((nz, 2, 128, 128), F32),
            vm((nz, RX, 128), F32),
            vm((2, half + 1, RX, 128), F32), vm((2, half + 1, 2, RC, 128), F32),
            vm((RC, 128), F32), vm((128, 128), F32), vm((64, 128), F32), vm((2, 64, 128), F32),
            vm((nf, 1, 128), F32),
            vm((64, 256), F32), vm((ni, 64 // ni, 256), F32), vm((64, 256), F32),
            vm((4, 64, 256), F32), vm((64, 256), F32),
            pltpu.SemaphoreType.REGULAR((3, 6)), dma((nz + 5,)), dma((nz,)), dma((nz,)), dma((ns, nz)), dma((ns, nz)),
            dma((ns, 2, half + 1)), dma((ns, 2, half + 1)), dma((2 + ns,)), dma((2 + ns,)),
            dma((nf,)), dma((nf,)), dma((2, ni)), dma((2, ni)), dma((2,)),
        ],
        compiler_params=pltpu.CompilerParams(collective_id=0, has_side_effects=True, vmem_limit_bytes=55091 << 10),
    )(act, cot, par, fm, sm, anc)
    new_first = 0.9 * fm[0] + 0.1 * clipped
    new_second = 0.95 * sm[0] + 0.05 * clipped * clipped
    new_mom = 0.9 * mom + mean_drift
    new_anc = anc - 0.7 * (mean_drift + 0.9 * new_mom)
    return new_anc, new_mom, new_first[None], new_second[None]


def solution(mesh):
    return jax.shard_map(
        shards,
        mesh=mesh,
        in_specs=(
            P("island", None, "fsdp", None),
            P("island", None, "fsdp", None),
            P("island", "fsdp", None),
            P("island", "fsdp", None),
            P("island", "fsdp", None),
            P("fsdp", None),
            P("fsdp", None),
        ),
        out_specs=(
            P("fsdp", None),
            P("fsdp", None),
            P("island", "fsdp", None),
            P("island", "fsdp", None),
        ),
        check_vma=False,
    )
```

```python
import functools

import jax
import jax.numpy as jnp
from jax import lax
from jax.experimental import pallas as pl
from jax.experimental.pallas import tpu as pltpu
from jax.sharding import PartitionSpec as P

MESH = pl.DeviceIdType.MESH
F32 = jnp.float32
STREAMS = ((0, 56, True, 1), (56, 112, True, -1), (112, 128, False, -1))
PRE, LAG, PZ, PA, PB, PC = 1, 4, 3, 4, 6, 7
RX = 112
RC = 128 - RX


def kernel(nz, ni, clip_limit, act, cot, par, fm, sm, anc, o_cl, o_md,
           a_v, c_v, ct, pp, h, pr, xv, ring_a, ring_c, xz, gt, gs, gb, ssl, dr, drr, md, st, res,
           word, ld_sem, cs, cr_sem, xs, xr, rs, rr, ms, mr, ss_s, ss_r, is_s, is_r, os):
    half = nz // 2
    i, f = lax.axis_index("island"), lax.axis_index("fsdp")
    z, x, c = f // 4, (f // 2) % 2, f % 2
    ox, oc = 1 - x, 1 - c
    rows = 128 // ni

    def dev(dz=0, xx=None, cc=None):
        zz = lax.rem(z + dz + nz, nz)
        return (i, zz * 4 + (x if xx is None else xx) * 2 + (c if cc is None else cc))

    def copy(src, dst, s, r, to):
        return pltpu.make_async_remote_copy(src_ref=src, dst_ref=dst, send_sem=s, recv_sem=r, device_id=to, device_id_type=MESH)

    barrier = pltpu.get_barrier_semaphore()

    def offset(k):
        return (2 * (k % 2) - 1) * (half - (k + 1) // 2)

    def load(k):
        zk = lax.rem(z + offset(k) + nz, nz)
        return pltpu.make_async_copy(act.at[0, :, :, pl.ds(pl.multiple_of(zk * 256, 256), 256)], a_v.at[k], ld_sem.at[k])

    def at_k(o):
        return 0 if abs(o) == half else 2 * (half - abs(o)) - (1 if o > 0 else 0)

    load_c = pltpu.make_async_copy(cot.at[0], c_v, ld_sem.at[nz])
    load_c.start()
    lax.fori_loop(0, nz, lambda k, _: (load(k).start(), 0)[1], 0)
    state = [pltpu.make_async_copy(src, st.at[n], ld_sem.at[nz + 1 + n])
             for n, src in enumerate((par.at[0], fm.at[0], sm.at[0], anc))]
    for s in state:
        s.start()

    yy, xp = i // 2, 2 * lax.rem(i, 2) + x

    def beside(dy, dx, dz):
        xq = lax.rem(xp + dx + 4, 4)
        return (lax.rem(yy + dy + ni // 2, ni // 2) * 2 + xq // 2, lax.rem(z + dz + nz, nz) * 4 + lax.rem(xq, 2) * 2 + c)

    sides = [beside(1, 0, 0), beside(-1, 0, 0), beside(0, 1, 0), beside(0, -1, 0), beside(0, 0, 1), beside(0, 0, -1)]
    for to in sides + [dev(cc=oc)]:
        pl.semaphore_signal(barrier, inc=1, device_id=to, device_id_type=MESH)

    def tell(r, which):
        for d in which:
            pl.semaphore_signal(word.at[r, d], inc=1, device_id=sides[d], device_id_type=MESH)

    def hear(r, which):
        for d in which:
            pl.semaphore_wait(word.at[r, d], 1)

    load_c.wait()
    for l in range(2):
        ct[l] = c_v[l].T

    first_x = [n for n, t in enumerate(STREAMS) if t[2]]
    last_x = [n for n, t in enumerate(STREAMS) if not t[2]]

    def core_copy(k):
        return copy(pp.at[k], pr.at[k], cs.at[k], cr_sem.at[k], dev(cc=oc))

    def x_copy(k, n):
        lo, hi = STREAMS[n][:2]
        return copy(h.at[k, ox, lo:hi], xv.at[k, lo:hi], xs.at[n, k], xr.at[n, k], dev(xx=ox))

    def product(k):
        load(k).wait()
        for l, out in ((oc, pp), (c, h)):
            p = jnp.dot(ct[l], a_v[k, l], preferred_element_type=F32)
            out[k, 0] = p[:, :128]
            out[k, 1] = p[:, 128:]

    def core_sum(k):
        core_copy(k).wait_recv()
        h[k] += pr[k]
        for n in first_x:
            x_copy(k, n).start()

    early = 2 * PRE + 1
    for k in range(early):
        product(k)
    pl.semaphore_wait(barrier, len(sides) + 1)
    tell(0, range(6))
    for k in range(early):
        core_copy(k).start()

    def longest(n, sign):
        return half if sign == STREAMS[n][3] else half - 1

    def landed(n, sign, o):
        lo, hi, first, _ = STREAMS[n]
        d = (sign + 1) // 2
        return ring_a.at[d, o, lo:hi] if first else ring_c.at[d, o, :, lo - RX:hi - RX]

    def ring(n, sign, o):
        lo, hi, first, _ = STREAMS[n]
        k = at_k(sign * o)
        d = (sign + 1) // 2
        src = h.at[k, x, lo:hi] if first else h.at[k, :, lo:hi]
        return copy(src, landed(n, sign, o), rs.at[n, d, o], rr.at[n, d, o], dev(dz=sign * (2 - o % 2)))

    def come(n, sign, o):
        total = None
        for d in (o + 2, o + 1):
            if d <= longest(n, sign):
                ring(n, sign, d).wait_recv()
                part = landed(n, sign, d)[...]
                total = part if total is None else total + part
        return total

    def pass_on(n, sign, o):
        lo, hi, first, _ = STREAMS[n]
        if o > longest(n, sign):
            return
        k = at_k(sign * o)
        t = come(n, sign, o) if o % 2 == 0 else None
        if first:
            x_copy(k, n).wait_recv()
            own = h[k, x, lo:hi] + xv[k, lo:hi]
            h[k, x, lo:hi] = own if t is None else own + t
        elif t is not None:
            h[k, :, lo:hi] += t
        ring(n, sign, o).start()

    def pass_all(which, o):
        for n in which:
            for sign in (1, -1):
                pass_on(n, sign, o)

    def group(g):
        return [0] if g == 0 else ([nz - 1] if g == half else [2 * g - 1, 2 * g])

    def produce(g):
        for k in group(g):
            if k >= early:
                product(k)
                core_copy(k).start()

    def collect(g):
        for k in group(g):
            core_sum(k)
        if (half - g) % 2:
            pass_all(last_x, half - g)

    for g in range(1, LAG + 1):
        produce(g)
    for g in range(half + 1):
        collect(g)
        if g + LAG < half:
            produce(g + LAG + 1)
        if g == PZ:
            hear(0, (4, 5))
            pass_all(last_x, half)
        if g == PA:
            pass_all(first_x, half)
        if g == PC:
            pass_all(last_x, half - 2)
        if g == PB:
            pass_all(first_x, half - 1)

    hear(0, range(4))
    tell(1, range(4))
    last = nz - 1
    zx = [copy(h.at[last, ox, STREAMS[n][0]:STREAMS[n][1]], xz.at[STREAMS[n][0] - RX:STREAMS[n][1] - RX],
               ms.at[2 + n], mr.at[2 + n], dev(xx=ox)) for n in last_x]
    for o in range(half - 2, 0, -1):
        if o == half // 2:
            hear(1, range(4))
            tell(2, range(4))
        if o % 2 == 0 and o < half - 2:
            pass_all(last_x, o)
        pass_all(first_x, o)
        if o == 2:
            for j, n in enumerate(last_x):
                lo, hi = STREAMS[n][:2]
                h[last, :, lo:hi] += come(n, 1, 0) + come(n, -1, 0)
                zx[j].start()
    for n in first_x:
        lo, hi = STREAMS[n][:2]
        x_copy(last, n).wait_recv()
        gt[lo:hi] = h[last, x, lo:hi] + xv[last, lo:hi] + come(n, 1, 0) + come(n, -1, 0)
    for c_x in zx:
        c_x.wait_recv()
    gt[RX:128] = h[last, x, RX:128] + xz[...]

    g = gt[...]
    ssl[0] = jnp.sum(g * g, axis=0, keepdims=True)

    def ss_copy(n):
        return copy(ssl.at[0], ssl.at[n], ss_s.at[0], ss_r.at[0], (i, lax.rem(f + n, 4 * nz)))

    def ss_start(n, _):
        ss_copy(2 * nz + n).start()
        ss_copy(2 * nz - n).start()
        return 0

    ss_copy(2 * nz).start()
    lax.fori_loop(1, 2 * nz, ss_start, 0)

    hear(2, range(4))
    gt[...] = g.T
    gs[...] = gt[pl.ds(pl.multiple_of(oc * 64, 64), 64)]
    gx = copy(gs, gb.at[c], ms.at[1], mr.at[1], dev(cc=oc))
    gx.start()
    gb[c] = gt[pl.ds(pl.multiple_of(c * 64, 64), 64)]
    for s in state:
        s.wait()

    def sent_k(k, _):
        core_copy(k).wait_send()
        for n in first_x:
            x_copy(k, n).wait_send()
        return 0

    lax.fori_loop(0, nz, sent_k, 0)
    for n in range(len(STREAMS)):
        for sign in (1, -1):
            for o in range(1, longest(n, sign) + 1):
                ring(n, sign, o).wait_send()
    for c_x in zx:
        c_x.wait_send()
    gx.wait_recv()
    gx.wait_send()

    all_ss = copy(ssl.at[1:4 * nz], ssl.at[1:4 * nz], ss_s.at[0], ss_r.at[0], dev(cc=oc))
    all_ss.wait_recv()
    squares = jnp.sum(jnp.sum(ssl[...], axis=0), axis=-1, keepdims=True)
    factor = jnp.minimum(1.0, clip_limit / (jnp.sqrt(squares) + 1e-06))

    for l in range(2):
        col = slice(l * 128, (l + 1) * 128)
        clipped = factor * gb[l]
        nf = 0.9 * st[1, :, col] + 0.1 * clipped
        ns = 0.95 * st[2, :, col] + 0.05 * clipped * clipped
        p = st[0, :, col]
        stepped = p - 0.05 * (nf / (jnp.sqrt(ns) + 1e-08) + 0.1 * p)
        dr[:, col] = st[3, :, col] - stepped
        res[:, col] = clipped

    outs = [pltpu.make_async_copy(src, dst, os.at[n]) for n, (src, dst) in enumerate(((res, o_cl), (md, o_md)))]

    mine = pl.ds(pl.multiple_of(yy * rows, rows), rows)

    def to_island(n):
        return (lax.rem(i + n, ni), f)

    def dr_copy(n):
        j = lax.rem(i + n, ni)
        return copy(dr.at[pl.ds(pl.multiple_of(j // 2 * rows, rows), rows)], drr.at[i], is_s.at[0, n], is_r.at[0, n], to_island(n))

    def md_copy(n):
        return copy(md.at[mine], md.at[mine], is_s.at[1, n], is_r.at[1, n], to_island(n))

    far = sorted(range(1, ni), key=lambda n: abs(n - ni // 2))
    for n in far:
        dr_copy(n).start()
    outs[0].start()
    all_ss.wait_send()
    drr[i] = dr[mine]
    for n in far:
        dr_copy(n).wait_recv()
    total = drr[0]
    for n in range(1, ni):
        total = total + drr[n]
    md[mine] = total / ni
    back = [n for n in far if n % 2 == 0]
    for n in back:
        md_copy(n).start()
    for n in back:
        md_copy(n).wait_recv()
    outs[1].start()

    for n in far:
        dr_copy(n).wait_send()
    for n in back:
        md_copy(n).wait_send()
    for o in outs:
        o.wait()


def shards(act, cot, par, fm, sm, anc, mom):
    nf, ni = lax.axis_size("fsdp"), lax.axis_size("island")
    nz = nf // 4
    half = nz // 2
    tok = act.shape[2]
    limit = 0.5 * float(act.shape[3] * 256) ** 0.5
    hbm = pl.BlockSpec(memory_space=pl.ANY)
    ns = len(STREAMS)
    vm, dma = pltpu.VMEM, pltpu.SemaphoreType.DMA
    clipped, mean_drift = pl.pallas_call(
        functools.partial(kernel, nz, ni, limit),
        out_shape=[jax.ShapeDtypeStruct(anc.shape, F32)] * 2,
        in_specs=[hbm] * 6,
        out_specs=[hbm] * 2,
        scratch_shapes=[
            vm((nz, 2, tok, 256), jnp.bfloat16), vm((2, tok, 128), jnp.bfloat16), vm((2, 128, tok), jnp.bfloat16),
            vm((nz, 2, 128, 128), F32), vm((nz, 2, 128, 128), F32), vm((nz, 2, 128, 128), F32),
            vm((nz, RX, 128), F32),
            vm((2, half + 1, RX, 128), F32), vm((2, half + 1, 2, RC, 128), F32),
            vm((RC, 128), F32), vm((128, 128), F32), vm((64, 128), F32), vm((2, 64, 128), F32),
            vm((nf, 1, 128), F32),
            vm((64, 256), F32), vm((ni, 128 // ni, 256), F32), vm((64, 256), F32),
            vm((4, 64, 256), F32), vm((64, 256), F32),
            pltpu.SemaphoreType.REGULAR((3, 6)), dma((nz + 5,)), dma((nz,)), dma((nz,)), dma((ns, nz)), dma((ns, nz)),
            dma((ns, 2, half + 1)), dma((ns, 2, half + 1)), dma((2 + ns,)), dma((2 + ns,)),
            dma((1,)), dma((1,)), dma((2, ni)), dma((2, ni)), dma((2,)),
        ],
        compiler_params=pltpu.CompilerParams(collective_id=0, has_side_effects=True, vmem_limit_bytes=55091 << 10),
    )(act, cot, par, fm, sm, anc)
    new_first = 0.9 * fm[0] + 0.1 * clipped
    new_second = 0.95 * sm[0] + 0.05 * clipped * clipped
    new_mom = 0.9 * mom + mean_drift
    new_anc = anc - 0.7 * (mean_drift + 0.9 * new_mom)
    return new_anc, new_mom, new_first[None], new_second[None]


def solution(mesh):
    return jax.shard_map(
        shards,
        mesh=mesh,
        in_specs=(
            P("island", None, "fsdp", None),
            P("island", None, "fsdp", None),
            P("island", "fsdp", None),
            P("island", "fsdp", None),
            P("island", "fsdp", None),
            P("fsdp", None),
            P("fsdp", None),
        ),
        out_specs=(
            P("fsdp", None),
            P("fsdp", None),
            P("island", "fsdp", None),
            P("island", "fsdp", None),
        ),
        check_vma=False,
    )
```

```python
import functools

import jax
import jax.numpy as jnp
from jax import lax
from jax.experimental import pallas as pl
from jax.experimental.pallas import tpu as pltpu
from jax.sharding import PartitionSpec as P

MESH = pl.DeviceIdType.MESH
F32 = jnp.float32
STREAMS = ((0, 56, True, 1), (56, 104, True, -1), (104, 128, False, -1))
PRE, LAG, PZ, PA, PB, PC = 1, 4, 3, 4, 6, 7
RX = 104
RC = 128 - RX


def kernel(nz, ni, clip_limit, act, cot, par, fm, sm, anc, o_cl, o_md,
           a_v, c_v, ct, pp, h, pr, xv, ring_a, ring_c, xz, gt, gs, gb, ssl, dr, drr, md, st, res,
           word, ld_sem, cs, cr_sem, xs, xr, rs, rr, ms, mr, ss_s, ss_r, is_s, is_r, os):
    half = nz // 2
    i, f = lax.axis_index("island"), lax.axis_index("fsdp")
    z, x, c = f // 4, (f // 2) % 2, f % 2
    ox, oc = 1 - x, 1 - c
    rows = 128 // ni

    def dev(dz=0, xx=None, cc=None):
        zz = lax.rem(z + dz + nz, nz)
        return (i, zz * 4 + (x if xx is None else xx) * 2 + (c if cc is None else cc))

    def copy(src, dst, s, r, to):
        return pltpu.make_async_remote_copy(src_ref=src, dst_ref=dst, send_sem=s, recv_sem=r, device_id=to, device_id_type=MESH)

    barrier = pltpu.get_barrier_semaphore()

    def offset(k):
        return (2 * (k % 2) - 1) * (half - (k + 1) // 2)

    def load(k):
        zk = lax.rem(z + offset(k) + nz, nz)
        return pltpu.make_async_copy(act.at[0, :, :, pl.ds(pl.multiple_of(zk * 256, 256), 256)], a_v.at[k], ld_sem.at[k])

    def at_k(o):
        return 0 if abs(o) == half else 2 * (half - abs(o)) - (1 if o > 0 else 0)

    load_c = pltpu.make_async_copy(cot.at[0], c_v, ld_sem.at[nz])
    yy, xp = i // 2, 2 * lax.rem(i, 2) + x

    def beside(dy, dx, dz):
        xq = lax.rem(xp + dx + 4, 4)
        return (lax.rem(yy + dy + ni // 2, ni // 2) * 2 + xq // 2, lax.rem(z + dz + nz, nz) * 4 + lax.rem(xq, 2) * 2 + c)

    sides = [beside(1, 0, 0), beside(-1, 0, 0), beside(0, 1, 0), beside(0, -1, 0), beside(0, 0, 1), beside(0, 0, -1)]
    for to in sides + [dev(cc=oc)]:
        pl.semaphore_signal(barrier, inc=1, device_id=to, device_id_type=MESH)

    load_c.start()
    lax.fori_loop(0, nz, lambda k, _: (load(k).start(), 0)[1], 0)
    def tell(r, which):
        for d in which:
            pl.semaphore_signal(word.at[r, d], inc=1, device_id=sides[d], device_id_type=MESH)

    def hear(r, which):
        for d in which:
            pl.semaphore_wait(word.at[r, d], 1)

    load_c.wait()
    for l in range(2):
        ct[l] = c_v[l].T

    first_x = [n for n, t in enumerate(STREAMS) if t[2]]
    last_x = [n for n, t in enumerate(STREAMS) if not t[2]]

    def core_copy(k):
        return copy(pp.at[k], pr.at[k], cs.at[k], cr_sem.at[k], dev(cc=oc))

    def x_copy(k, n):
        lo, hi = STREAMS[n][:2]
        return copy(h.at[k, ox, lo:hi], xv.at[k, lo:hi], xs.at[n, k], xr.at[n, k], dev(xx=ox))

    def product(k):
        load(k).wait()
        for l, out in ((oc, pp), (c, h)):
            p = jnp.dot(ct[l], a_v[k, l], preferred_element_type=F32)
            out[k, 0] = p[:, :128]
            out[k, 1] = p[:, 128:]

    def core_sum(k):
        core_copy(k).wait_recv()
        h[k] += pr[k]
        for n in first_x:
            x_copy(k, n).start()

    early = 2 * PRE + 1
    for k in range(early):
        product(k)
    pl.semaphore_wait(barrier, len(sides) + 1)
    tell(0, range(6))
    for k in range(early):
        core_copy(k).start()

    def longest(n, sign):
        return half if sign == STREAMS[n][3] else half - 1

    def landed(n, sign, o):
        lo, hi, first, _ = STREAMS[n]
        d = (sign + 1) // 2
        return ring_a.at[d, o, lo:hi] if first else ring_c.at[d, o, :, lo - RX:hi - RX]

    def ring(n, sign, o):
        lo, hi, first, _ = STREAMS[n]
        k = at_k(sign * o)
        d = (sign + 1) // 2
        src = h.at[k, x, lo:hi] if first else h.at[k, :, lo:hi]
        return copy(src, landed(n, sign, o), rs.at[n, d, o], rr.at[n, d, o], dev(dz=sign * (2 - o % 2)))

    def come(n, sign, o):
        total = None
        for d in (o + 2, o + 1):
            if d <= longest(n, sign):
                ring(n, sign, d).wait_recv()
                part = landed(n, sign, d)[...]
                total = part if total is None else total + part
        return total

    def pass_on(n, sign, o):
        lo, hi, first, _ = STREAMS[n]
        if o > longest(n, sign):
            return
        k = at_k(sign * o)
        t = come(n, sign, o) if o % 2 == 0 else None
        if first:
            x_copy(k, n).wait_recv()
            own = h[k, x, lo:hi] + xv[k, lo:hi]
            h[k, x, lo:hi] = own if t is None else own + t
        elif t is not None:
            h[k, :, lo:hi] += t
        ring(n, sign, o).start()

    def pass_all(which, o):
        for n in which:
            for sign in (1, -1):
                pass_on(n, sign, o)

    def group(g):
        return [0] if g == 0 else ([nz - 1] if g == half else [2 * g - 1, 2 * g])

    def produce(g):
        for k in group(g):
            if k >= early:
                product(k)
                core_copy(k).start()

    def collect(g):
        for k in group(g):
            core_sum(k)
        if (half - g) % 2:
            pass_all(last_x, half - g)

    for g in range(1, LAG + 1):
        produce(g)
    for g in range(half + 1):
        collect(g)
        if g + LAG < half:
            produce(g + LAG + 1)
        if g == PZ:
            hear(0, (4, 5))
            pass_all(last_x, half)
        if g == PA:
            pass_all(first_x, half)
        if g == PC:
            pass_all(last_x, half - 2)
        if g == PB:
            pass_all(first_x, half - 1)

    state = [pltpu.make_async_copy(src, st.at[n], ld_sem.at[nz + 1 + n])
             for n, src in enumerate((par.at[0], fm.at[0], sm.at[0], anc))]
    for s in state:
        s.start()
    hear(0, range(4))
    tell(1, range(4))
    last = nz - 1
    zx = [copy(h.at[last, ox, STREAMS[n][0]:STREAMS[n][1]], xz.at[STREAMS[n][0] - RX:STREAMS[n][1] - RX],
               ms.at[2 + n], mr.at[2 + n], dev(xx=ox)) for n in last_x]
    for o in range(half - 2, 0, -1):
        if o == half // 2:
            hear(1, range(4))
            tell(2, range(4))
        if o % 2 == 0 and o < half - 2:
            pass_all(last_x, o)
        pass_all(first_x, o)
        if o == 1:
            for j, n in enumerate(last_x):
                lo, hi = STREAMS[n][:2]
                h[last, :, lo:hi] += come(n, 1, 0) + come(n, -1, 0)
                zx[j].start()
    for n in first_x:
        lo, hi = STREAMS[n][:2]
        x_copy(last, n).wait_recv()
        gt[lo:hi] = h[last, x, lo:hi] + xv[last, lo:hi] + come(n, 1, 0) + come(n, -1, 0)
    for c_x in zx:
        c_x.wait_recv()
    gt[RX:128] = h[last, x, RX:128] + xz[...]

    g = gt[...]
    ssl[0] = jnp.sum(g * g, axis=0, keepdims=True)

    def ss_copy(n):
        return copy(ssl.at[0], ssl.at[n], ss_s.at[0], ss_r.at[0], (i, lax.rem(f + n, 4 * nz)))

    def ss_start(n, _):
        ss_copy(2 * nz + n).start()
        ss_copy(2 * nz - n).start()
        return 0

    ss_copy(2 * nz).start()
    lax.fori_loop(1, 2 * nz, ss_start, 0)

    hear(2, range(4))
    gt[...] = g.T
    gs[...] = gt[pl.ds(pl.multiple_of(oc * 64, 64), 64)]
    gx = copy(gs, gb.at[c], ms.at[1], mr.at[1], dev(cc=oc))
    gx.start()
    gb[c] = gt[pl.ds(pl.multiple_of(c * 64, 64), 64)]
    for s in state:
        s.wait()

    def sent_k(k, _):
        core_copy(k).wait_send()
        for n in first_x:
            x_copy(k, n).wait_send()
        return 0

    lax.fori_loop(0, nz, sent_k, 0)
    for n in range(len(STREAMS)):
        for sign in (1, -1):
            for o in range(1, longest(n, sign) + 1):
                ring(n, sign, o).wait_send()
    for c_x in zx:
        c_x.wait_send()
    gx.wait_recv()
    gx.wait_send()

    all_ss = copy(ssl.at[1:4 * nz], ssl.at[1:4 * nz], ss_s.at[0], ss_r.at[0], dev(cc=oc))
    all_ss.wait_recv()
    squares = jnp.sum(jnp.sum(ssl[...], axis=0), axis=-1, keepdims=True)
    factor = jnp.minimum(1.0, clip_limit / (jnp.sqrt(squares) + 1e-06))

    for l in range(2):
        col = slice(l * 128, (l + 1) * 128)
        clipped = factor * gb[l]
        nf = 0.9 * st[1, :, col] + 0.1 * clipped
        ns = 0.95 * st[2, :, col] + 0.05 * clipped * clipped
        p = st[0, :, col]
        stepped = p - 0.05 * (nf / (jnp.sqrt(ns) + 1e-08) + 0.1 * p)
        dr[:, col] = st[3, :, col] - stepped
        res[:, col] = clipped

    outs = [pltpu.make_async_copy(src, dst, os.at[n]) for n, (src, dst) in enumerate(((res, o_cl), (md, o_md)))]

    mine = pl.ds(pl.multiple_of(yy * rows, rows), rows)

    def to_island(n):
        return (lax.rem(i + n, ni), f)

    def dr_copy(n):
        j = lax.rem(i + n, ni)
        return copy(dr.at[pl.ds(pl.multiple_of(j // 2 * rows, rows), rows)], drr.at[i], is_s.at[0, n], is_r.at[0, n], to_island(n))

    def md_copy(n):
        return copy(md.at[mine], md.at[mine], is_s.at[1, n], is_r.at[1, n], to_island(n))

    far = sorted(range(1, ni), key=lambda n: abs(n - ni // 2))
    for n in far:
        dr_copy(n).start()
    outs[0].start()
    all_ss.wait_send()
    drr[i] = dr[mine]
    for n in far:
        dr_copy(n).wait_recv()
    total = drr[0]
    for n in range(1, ni):
        total = total + drr[n]
    md[mine] = total / ni
    back = [n for n in far if n % 2 == 0]
    for n in back:
        md_copy(n).start()
    for n in back:
        md_copy(n).wait_recv()
    outs[1].start()

    for n in far:
        dr_copy(n).wait_send()
    for n in back:
        md_copy(n).wait_send()
    for o in outs:
        o.wait()


def shards(act, cot, par, fm, sm, anc, mom):
    nf, ni = lax.axis_size("fsdp"), lax.axis_size("island")
    nz = nf // 4
    half = nz // 2
    tok = act.shape[2]
    limit = 0.5 * float(act.shape[3] * 256) ** 0.5
    hbm = pl.BlockSpec(memory_space=pl.ANY)
    ns = len(STREAMS)
    vm, dma = pltpu.VMEM, pltpu.SemaphoreType.DMA
    clipped, mean_drift = pl.pallas_call(
        functools.partial(kernel, nz, ni, limit),
        out_shape=[jax.ShapeDtypeStruct(anc.shape, F32)] * 2,
        in_specs=[hbm] * 6,
        out_specs=[hbm] * 2,
        scratch_shapes=[
            vm((nz, 2, tok, 256), jnp.bfloat16), vm((2, tok, 128), jnp.bfloat16), vm((2, 128, tok), jnp.bfloat16),
            vm((nz, 2, 128, 128), F32), vm((nz, 2, 128, 128), F32), vm((nz, 2, 128, 128), F32),
            vm((nz, RX, 128), F32),
            vm((2, half + 1, RX, 128), F32), vm((2, half + 1, 2, RC, 128), F32),
            vm((RC, 128), F32), vm((128, 128), F32), vm((64, 128), F32), vm((2, 64, 128), F32),
            vm((nf, 1, 128), F32),
            vm((64, 256), F32), vm((ni, 128 // ni, 256), F32), vm((64, 256), F32),
            vm((4, 64, 256), F32), vm((64, 256), F32),
            pltpu.SemaphoreType.REGULAR((3, 6)), dma((nz + 5,)), dma((nz,)), dma((nz,)), dma((ns, nz)), dma((ns, nz)),
            dma((ns, 2, half + 1)), dma((ns, 2, half + 1)), dma((2 + ns,)), dma((2 + ns,)),
            dma((1,)), dma((1,)), dma((2, ni)), dma((2, ni)), dma((2,)),
        ],
        compiler_params=pltpu.CompilerParams(collective_id=0, has_side_effects=True, vmem_limit_bytes=55091 << 10),
    )(act, cot, par, fm, sm, anc)
    new_first = 0.9 * fm[0] + 0.1 * clipped
    new_second = 0.95 * sm[0] + 0.05 * clipped * clipped
    new_mom = 0.9 * mom + mean_drift
    new_anc = anc - 0.7 * (mean_drift + 0.9 * new_mom)
    return new_anc, new_mom, new_first[None], new_second[None]


def solution(mesh):
    return jax.shard_map(
        shards,
        mesh=mesh,
        in_specs=(
            P("island", None, "fsdp", None),
            P("island", None, "fsdp", None),
            P("island", "fsdp", None),
            P("island", "fsdp", None),
            P("island", "fsdp", None),
            P("fsdp", None),
            P("fsdp", None),
        ),
        out_specs=(
            P("fsdp", None),
            P("fsdp", None),
            P("island", "fsdp", None),
            P("island", "fsdp", None),
        ),
        check_vma=False,
    )
```
